32 devices in a mesh: obs: 8 (over z, x), tile: 4 (over y, core).
Axes of the slice: x: 2, y: 2, z: 4, core: 2. Of those that a mesh axis runs over, the one named last changes fastest.
Arguments:
- jacobian: bfloat16 [2048, 65536], P(('obs', 'tile')), may hold values from -0.5 to 0.5
- obs_weight: float32 [2048], P(('obs', 'tile')), may hold values from 0.1 to 10
- block_order: int32 [512], replicated, may hold values from 0 to 511, each once
- tile_pairs: int32 [8, 64, 2], P('obs'), may hold values from 0 to 63, as said below
- tile_count: int32 [8], P('obs'), may hold values from 1 to 64, as said below
Outputs:
- hessian: float32 [512, 128, 128], P(('obs', 'tile'))
The draws below stay inside these ranges and needn't reach their ends.
Inputs may be any that keep to these rules, and one draw needn't show every extreme that they name: `tile_pairs`: slot numbers within an owner's own 64 slots; the first tile_count[j] pairs of owner j are distinct. `tile_count`: some owner has 64 live tiles.
All inputs are finite; a program needn't handle non-finite values.
Results may differ from the reference program's by a relative error of at most 0.0015.
Values may be sent and summed in bfloat16 or wider, within the bound.
A program may use at most 256 MiB of HBM per device.

```python
import math
import jax
import jax.numpy as jnp
from jax import lax

ZONES = 65536
BLOCK = 128
TILE_MAX = 64
OBS_ROWS = 2048
ZBLOCKS = 512
OWNERS = 8
ZB_DEV = 64


def draw_tile_count(key, part):
    first_key, second_key = jax.random.split(jax.random.fold_in(key, 11))
    counts = jax.random.randint(first_key, (OWNERS,), max(1, TILE_MAX // 8), TILE_MAX // 2 + 1, dtype=jnp.int32)
    busiest = jax.random.randint(second_key, (), 0, OWNERS, dtype=jnp.int32)
    return jnp.where(jnp.arange(OWNERS, dtype=jnp.int32) == busiest, TILE_MAX, counts).astype(jnp.int32)


def pick_pairs(owner_key):
    return jax.random.permutation(owner_key, ZB_DEV * ZB_DEV)[:TILE_MAX]


def draw_tile_pairs(key, part):
    owner_keys = jax.random.split(jax.random.fold_in(key, 23), OWNERS)
    orders = jax.vmap(pick_pairs)(owner_keys).astype(jnp.int32)
    return jnp.stack([orders // ZB_DEV, orders % ZB_DEV], axis=-1).astype(jnp.int32)


def levels(rng, dims, pieces, smallest, high):
    gain, own = 1.0, jax.random.fold_in(rng, 6)
    for position, shards_of in pieces:
        steps = jnp.exp(jax.random.uniform(jax.random.fold_in(own, position), (shards_of,), jnp.float32, smallest / len(pieces), high / len(pieces)))
        gain = gain * jnp.repeat(steps, dims[position] // shards_of).reshape([-1 if axis == position else 1 for axis in range(len(dims))])
    return gain


def centred(key, shape, scale, bound, cuts=(), held_as=jnp.bfloat16):
    gain = levels(key, shape, cuts, -0.22, 0.18) if cuts else 1.0
    entries = jax.random.normal(key, shape, jnp.float32) * scale * gain
    return jnp.minimum(jnp.maximum(entries, -bound), bound).astype(held_as)


def setup_inputs(seed: int = 0) -> dict:
    arg_keys = jax.random.split(jax.random.key(seed), 6)
    jacobian = centred(arg_keys[0], (OBS_ROWS, ZONES), (OBS_ROWS // 16) ** -0.5, 0.5, ((0, 32),))
    obs_weight = jnp.clip(jnp.exp(math.log(10.0) - 4.6051702 * jax.random.uniform(arg_keys[1], (OBS_ROWS,), jnp.float32) ** levels(arg_keys[1], (OBS_ROWS,), ((0, 32),), -0.2, 0.2)), 0.1, 10.0)
    block_order = jax.random.permutation(arg_keys[2], ZBLOCKS).astype(jnp.int32)
    tile_pairs = draw_tile_pairs(jax.random.fold_in(arg_keys[5], 71), 0)
    tile_count = draw_tile_count(jax.random.fold_in(arg_keys[5], 71), 0)
    return dict(jacobian=jacobian, obs_weight=obs_weight, block_order=block_order, tile_pairs=tile_pairs, tile_count=tile_count)


def reference(jacobian, obs_weight, block_order, tile_pairs, tile_count):
    root_weight = jnp.sqrt(obs_weight)[:, None]

    def column_block(slot_index):
        zone_block = block_order[slot_index]
        column_piece = lax.dynamic_slice_in_dim(jacobian, (zone_block * BLOCK).astype(jnp.int32), BLOCK, 1)
        return (column_piece.astype(jnp.float32) * root_weight).astype(jnp.bfloat16)

    def owner_tiles(owner_index):

        def one_tile(tile_index):

            def compute(unused):
                left_block = column_block(owner_index * ZB_DEV + tile_pairs[owner_index, tile_index, 0])
                right_block = column_block(owner_index * ZB_DEV + tile_pairs[owner_index, tile_index, 1])
                return lax.dot_general(left_block, right_block, (((0,), (0,)), ((), ())), preferred_element_type=jnp.float32)

            def empty_tile(unused):
                return jnp.zeros((BLOCK, BLOCK), jnp.float32)
            return lax.cond(tile_index < tile_count[owner_index], compute, empty_tile, 0)
        return lax.map(one_tile, jnp.arange(TILE_MAX, dtype=jnp.int32))
    tiles = lax.map(owner_tiles, jnp.arange(OWNERS, dtype=jnp.int32))
    return tiles.reshape(OWNERS * TILE_MAX, BLOCK, BLOCK)
```

```python
import functools
import jax
import jax.numpy as jnp
from jax import lax
from jax.experimental import pallas as pl
from jax.experimental.pallas import tpu as pltpu
from jax.sharding import Mesh, PartitionSpec as P

BLOCK = 128
PARTS = 2


def order_kernel(slots, parts, per_part, order_ref, jac_ref, weight_ref, out_ref):
    dest, part = pl.program_id(0), pl.program_id(1)
    first = (part * per_part + dest) * slots
    weight = jnp.broadcast_to(weight_ref[...], (weight_ref.shape[0], BLOCK))

    def one(slot, carry):
        start = pl.multiple_of(order_ref[first + slot] * BLOCK, BLOCK)
        piece = jac_ref[:, pl.ds(start, BLOCK)].astype(jnp.float32) * weight
        out_ref[0, 0, slot] = piece.astype(jnp.bfloat16)
        return carry

    lax.fori_loop(0, slots, one, 0, unroll=4)


def order_columns(jacobian, root_weight, block_order, parts, per_part):
    rows, width = jacobian.shape
    slots = block_order.shape[0] // (parts * per_part)
    return pl.pallas_call(
        functools.partial(order_kernel, slots, parts, per_part),
        out_shape=jax.ShapeDtypeStruct((per_part, parts, slots, rows, BLOCK), jnp.bfloat16),
        grid_spec=pltpu.PrefetchScalarGridSpec(
            num_scalar_prefetch=1,
            grid=(per_part, parts),
            in_specs=[
                pl.BlockSpec((rows, width), lambda d, p, order: (0, 0)),
                pl.BlockSpec((rows, 1), lambda d, p, order: (0, 0)),
            ],
            out_specs=pl.BlockSpec((1, 1, slots, rows, BLOCK), lambda d, p, order: (d, p, 0, 0, 0)),
        ),
        compiler_params=pltpu.CompilerParams(vmem_limit_bytes=48 << 20),
    )(block_order, jacobian, root_weight)


def tile_kernel(group, pairs_ref, count_ref, cols_ref, out_ref):
    part, step = pl.program_id(0), pl.program_id(1)
    senders, slots, rows = cols_ref.shape[0], cols_ref.shape[2], cols_ref.shape[3]

    def one(index, carry):
        tile = step * group + index

        @pl.when(tile < count_ref[part])
        def _():
            a = pairs_ref[part, 2 * tile]
            b = pairs_ref[part, 2 * tile + 1]
            left = cols_ref[:, 0, a].reshape(senders * rows, BLOCK)
            right = cols_ref[:, 0, b].reshape(senders * rows, BLOCK)
            out_ref[0, index] = lax.dot_general(
                left, right, (((0,), (0,)), ((), ())), preferred_element_type=jnp.float32
            )

        @pl.when(tile >= count_ref[part])
        def _():
            out_ref[0, index] = jnp.zeros((BLOCK, BLOCK), jnp.float32)

        return carry

    lax.fori_loop(0, group, one, 0)


def partial_tiles(columns, pairs, counts):
    senders, parts, slots, rows, _ = columns.shape
    tiles = pairs.shape[1]
    group = 16
    return pl.pallas_call(
        functools.partial(tile_kernel, group),
        out_shape=jax.ShapeDtypeStruct((parts, tiles, BLOCK, BLOCK), jnp.float32),
        grid_spec=pltpu.PrefetchScalarGridSpec(
            num_scalar_prefetch=2,
            grid=(parts, tiles // group),
            in_specs=[
                pl.BlockSpec((senders, 1, slots, rows, BLOCK), lambda p, g, pr, ct: (0, p, 0, 0, 0)),
            ],
            out_specs=pl.BlockSpec((1, group, BLOCK, BLOCK), lambda p, g, pr, ct: (p, g, 0, 0)),
        ),
        compiler_params=pltpu.CompilerParams(vmem_limit_bytes=48 << 20),
    )(pairs.reshape(parts, tiles * 2), counts, columns)


def body(parts, per_part, jacobian, obs_weight, block_order, tile_pairs, tile_count):
    root_weight = jnp.sqrt(obs_weight)[:, None]
    outgoing = order_columns(jacobian, root_weight, block_order, parts, per_part)
    arrived = lax.all_to_all(outgoing, "obs", split_axis=0, concat_axis=0, tiled=True)
    live = jnp.broadcast_to(tile_count[:, None, None], (1, 1, 2))
    listed = jnp.concatenate([tile_pairs, live], axis=1)
    if parts > 1:
        listed = lax.all_gather(listed, "part", axis=0, tiled=True)
    tiles = partial_tiles(arrived, listed[:, :-1], listed[:, -1, 0])
    tiles = tiles.reshape(-1, BLOCK, BLOCK)
    axes = ("part", "tile") if parts > 1 else "tile"
    return lax.psum_scatter(tiles, axes, scatter_dimension=0, tiled=True)


def solution(mesh):
    owners, tile_size = mesh.devices.shape
    parts = PARTS if owners % PARTS == 0 else 1
    per_part = owners // parts
    devices = mesh.devices.reshape(parts, per_part, tile_size)
    split_mesh = Mesh(devices, ("part", "obs", "tile"))
    every = ("part", "obs", "tile")
    return jax.shard_map(
        functools.partial(body, parts, per_part),
        mesh=split_mesh,
        in_specs=(P(every, None), P(every), P(), P(("part", "obs"), None, None), P(("part", "obs"))),
        out_specs=P(every, None, None),
        check_vma=False,
    )
```

```python
import functools
import jax
import jax.numpy as jnp
from jax import lax
from jax.experimental import pallas as pl
from jax.experimental.pallas import tpu as pltpu
from jax.sharding import Mesh, PartitionSpec as P

BLOCK = 128
PARTS = 2


def order_kernel(slots, parts, per_part, order_ref, jac_ref, weight_ref, out_ref):
    dest, part = pl.program_id(0), pl.program_id(1)
    first = (part * per_part + dest) * slots
    weight = jnp.broadcast_to(weight_ref[...], (weight_ref.shape[0], BLOCK))

    def one(slot, carry):
        start = pl.multiple_of(order_ref[first + slot] * BLOCK, BLOCK)
        piece = jac_ref[:, pl.ds(start, BLOCK)].astype(jnp.float32) * weight
        out_ref[0, 0, slot] = piece.astype(jnp.bfloat16)
        return carry

    lax.fori_loop(0, slots, one, 0, unroll=4)


def order_columns(jacobian, root_weight, block_order, parts, per_part):
    rows, width = jacobian.shape
    slots = block_order.shape[0] // (parts * per_part)
    return pl.pallas_call(
        functools.partial(order_kernel, slots, parts, per_part),
        out_shape=jax.ShapeDtypeStruct((per_part, parts, slots, rows, BLOCK), jnp.bfloat16),
        grid_spec=pltpu.PrefetchScalarGridSpec(
            num_scalar_prefetch=1,
            grid=(per_part, parts),
            in_specs=[
                pl.BlockSpec((rows, width), lambda d, p, order: (0, 0)),
                pl.BlockSpec((rows, 1), lambda d, p, order: (0, 0)),
            ],
            out_specs=pl.BlockSpec((1, 1, slots, rows, BLOCK), lambda d, p, order: (d, p, 0, 0, 0)),
        ),
        compiler_params=pltpu.CompilerParams(vmem_limit_bytes=48 << 20),
    )(block_order, jacobian, root_weight)


def tile_kernel(group, pairs_ref, count_ref, cols_ref, out_ref):
    part, step = pl.program_id(0), pl.program_id(1)
    senders, slots, rows = cols_ref.shape[0], cols_ref.shape[2], cols_ref.shape[3]

    def one(index, carry):
        tile = step * group + index

        @pl.when(tile < count_ref[part])
        def _():
            a = pairs_ref[part, 2 * tile]
            b = pairs_ref[part, 2 * tile + 1]
            left = cols_ref[:, 0, a].reshape(senders * rows, BLOCK)
            right = cols_ref[:, 0, b].reshape(senders * rows, BLOCK)
            out_ref[0, index] = lax.dot_general(
                left, right, (((0,), (0,)), ((), ())), preferred_element_type=jnp.float32
            )

        @pl.when(tile >= count_ref[part])
        def _():
            out_ref[0, index] = jnp.zeros((BLOCK, BLOCK), jnp.float32)

        return carry

    lax.fori_loop(0, group, one, 0)


def partial_tiles(columns, pairs, counts):
    senders, parts, slots, rows, _ = columns.shape
    tiles = pairs.shape[1]
    group = 16
    return pl.pallas_call(
        functools.partial(tile_kernel, group),
        out_shape=jax.ShapeDtypeStruct((parts, tiles, BLOCK, BLOCK), jnp.float32),
        grid_spec=pltpu.PrefetchScalarGridSpec(
            num_scalar_prefetch=2,
            grid=(parts, tiles // group),
            in_specs=[
                pl.BlockSpec((senders, 1, slots, rows, BLOCK), lambda p, g, pr, ct: (0, p, 0, 0, 0)),
            ],
            out_specs=pl.BlockSpec((1, group, BLOCK, BLOCK), lambda p, g, pr, ct: (p, g, 0, 0)),
        ),
        compiler_params=pltpu.CompilerParams(vmem_limit_bytes=48 << 20),
    )(pairs.reshape(parts, tiles * 2), counts, columns)


def part_tiles(columns, listed):
    tiles = partial_tiles(columns, listed[:, :-1], listed[:, -1, 0])
    return tiles.reshape(-1, BLOCK, BLOCK)


def body(parts, per_part, jacobian, obs_weight, block_order, tile_pairs, tile_count):
    root_weight = jnp.sqrt(obs_weight)[:, None]
    live = jnp.broadcast_to(tile_count[:, None, None], (1, 1, 2))
    listed = jnp.concatenate([tile_pairs, live], axis=1)
    swap = [(0, 1), (1, 0)]
    here = lax.axis_index("part")
    orders = block_order.reshape(parts, -1)
    own_order = lax.dynamic_index_in_dim(orders, here, 0, keepdims=False)
    far_order = lax.dynamic_index_in_dim(orders, 1 - here, 0, keepdims=False)

    far_listed = lax.ppermute(listed, "part", swap)
    far_out = order_columns(jacobian, root_weight, far_order, 1, per_part)
    far_out, far_listed = lax.optimization_barrier((far_out, far_listed))
    far_columns = lax.all_to_all(far_out, "obs", split_axis=0, concat_axis=0, tiled=True)
    own_out = order_columns(jacobian, root_weight, own_order, 1, per_part)
    far_columns, own_out = lax.optimization_barrier((far_columns, own_out))
    own_columns = lax.all_to_all(own_out, "obs", split_axis=0, concat_axis=0, tiled=True)

    far_sum = lax.psum_scatter(part_tiles(far_columns, far_listed), "tile", scatter_dimension=0, tiled=True)
    from_far = lax.ppermute(far_sum, "part", swap)
    own_sum = lax.psum_scatter(part_tiles(own_columns, listed), "tile", scatter_dimension=0, tiled=True)
    return own_sum + from_far


def solution(mesh):
    owners, tile_size = mesh.devices.shape
    parts = PARTS
    per_part = owners // parts
    devices = mesh.devices.reshape(parts, per_part, tile_size)
    split_mesh = Mesh(devices, ("part", "obs", "tile"))
    every = ("part", "obs", "tile")
    return jax.shard_map(
        functools.partial(body, parts, per_part),
        mesh=split_mesh,
        in_specs=(P(every, None), P(every), P(), P(("part", "obs"), None, None), P(("part", "obs"))),
        out_specs=P(every, None, None),
        check_vma=False,
    )
```

```python
import functools
import jax
import jax.numpy as jnp
from jax import lax
from jax.experimental import pallas as pl
from jax.experimental.pallas import tpu as pltpu
from jax.sharding import Mesh, PartitionSpec as P

BLOCK = 128
PARTS = 2


def order_kernel(slots, parts, per_part, order_ref, jac_ref, weight_ref, out_ref):
    dest, part = pl.program_id(0), pl.program_id(1)
    first = (part * per_part + dest) * slots
    weight = jnp.broadcast_to(weight_ref[...], (weight_ref.shape[0], BLOCK))

    def one(slot, carry):
        start = pl.multiple_of(order_ref[first + slot] * BLOCK, BLOCK)
        piece = jac_ref[:, pl.ds(start, BLOCK)].astype(jnp.float32) * weight
        out_ref[0, 0, slot] = piece.astype(jnp.bfloat16)
        return carry

    lax.fori_loop(0, slots, one, 0, unroll=4)


def order_columns(jacobian, root_weight, block_order, parts, per_part):
    rows, width = jacobian.shape
    slots = block_order.shape[0] // (parts * per_part)
    return pl.pallas_call(
        functools.partial(order_kernel, slots, parts, per_part),
        out_shape=jax.ShapeDtypeStruct((per_part, parts, slots, rows, BLOCK), jnp.bfloat16),
        grid_spec=pltpu.PrefetchScalarGridSpec(
            num_scalar_prefetch=1,
            grid=(per_part, parts),
            in_specs=[
                pl.BlockSpec((rows, width), lambda d, p, order: (0, 0)),
                pl.BlockSpec((rows, 1), lambda d, p, order: (0, 0)),
            ],
            out_specs=pl.BlockSpec((1, 1, slots, rows, BLOCK), lambda d, p, order: (d, p, 0, 0, 0)),
        ),
        compiler_params=pltpu.CompilerParams(vmem_limit_bytes=48 << 20),
    )(block_order, jacobian, root_weight)


def kernel(n, rows, quarter, own_list, far_list, sent_ref, out_ref,
           far_cols, own_cols, far_tiles, own_tiles, pair_in, side_in, part_in,
           far_ss, far_rs, own_ss, own_rs, pair_ss, pair_rs, side_ss, side_rs, part_ss, part_rs):
    part, me, t = lax.axis_index("part"), lax.axis_index("obs"), lax.axis_index("tile")
    hi, lo = t // 2, t % 2
    pair_peer = {"tile": hi * 2 + (1 - lo)}
    side_peer = {"tile": (1 - hi) * 2 + lo}
    part_peer = {"part": 1 - part}
    peers = [{"obs": (me + d) % n} for d in range(n)]
    mesh_id = pl.DeviceIdType.MESH

    barrier = pltpu.get_barrier_semaphore()
    for peer in peers[1:] + [pair_peer, side_peer, part_peer]:
        pl.semaphore_signal(barrier, inc=1, device_id=peer, device_id_type=mesh_id)

    def send(source, target, ss, rs, peer):
        return pltpu.make_async_remote_copy(
            src_ref=source, dst_ref=target, send_sem=ss, recv_sem=rs,
            device_id=peer, device_id_type=mesh_id)

    far_moves, own_moves = [None], [None]
    for d in range(1, n):
        dest = (me + d) % n
        place = pl.ds(d * rows, rows)
        far_moves.append(
            send(sent_ref.at[dest, 0], far_cols.at[:, place], far_ss.at[d], far_rs.at[d], peers[d]))
        own_moves.append(
            send(sent_ref.at[dest, 1], own_cols.at[:, place], own_ss.at[d], own_rs.at[d], peers[d]))
    far_kept = pltpu.make_async_copy(sent_ref.at[me, 0], far_cols.at[:, pl.ds(0, rows)], far_ss.at[0])
    own_kept = pltpu.make_async_copy(sent_ref.at[me, 1], own_cols.at[:, pl.ds(0, rows)], own_ss.at[0])
    pl.semaphore_wait(barrier, n + 2)
    for d in range(1, n):
        far_moves[d].start()
    far_kept.start()
    own_kept.start()
    for d in range(1, n):
        far_moves[d].wait_send()
        own_moves[d].start()
    far_kept.wait()
    own_kept.wait()

    def products(listed, columns, tiles, q, place):
        def one(i, carry):
            tile = q * quarter + i
            left = columns[listed[2 * tile]]
            right = columns[listed[2 * tile + 1]]
            tiles[place, i] = lax.dot_general(
                left, right, (((0,), (0,)), ((), ())), preferred_element_type=jnp.float32)
            return carry

        lax.fori_loop(0, quarter, one, 0, unroll=2)

    def reduce(phase, listed, columns, tiles):
        near = [send(tiles.at[2 * i], pair_in.at[phase, i], pair_ss.at[phase, i],
                     pair_rs.at[phase, i], pair_peer) for i in range(2)]
        side = send(tiles.at[1], side_in.at[phase], side_ss.at[phase], side_rs.at[phase], side_peer)
        products(listed, columns, tiles, (1 - hi) * 2 + (1 - lo), 0)
        near[0].start()
        products(listed, columns, tiles, (1 - hi) * 2 + lo, 1)
        near[0].wait_recv()
        tiles[1] = tiles[1] + pair_in[phase, 0]
        side.start()
        products(listed, columns, tiles, hi * 2 + (1 - lo), 2)
        near[1].start()
        products(listed, columns, tiles, hi * 2 + lo, 3)
        near[1].wait_recv()
        tiles[3] = tiles[3] + pair_in[phase, 1]
        return near, side

    for d in range(1, n):
        far_moves[d].wait_recv()
    far_near, far_side = reduce(0, far_list, far_cols, far_tiles)
    far_side.wait_recv()
    far_tiles[3] = far_tiles[3] + side_in[0]
    across = send(far_tiles.at[3], part_in, part_ss, part_rs, part_peer)
    across.start()
    for d in range(1, n):
        own_moves[d].wait_recv()
    own_near, own_side = reduce(1, own_list, own_cols, own_tiles)
    across.wait_recv()
    own_tiles[3] = own_tiles[3] + part_in[...]
    own_side.wait_recv()
    out_ref[...] = own_tiles[3] + side_in[1]
    for d in range(1, n):
        own_moves[d].wait_send()
    for move in far_near + own_near + [far_side, own_side, across]:
        move.wait_send()


def body(n, jacobian, obs_weight, block_order, tile_pairs, tile_count):
    rows, width = jacobian.shape
    slots = block_order.shape[0] // (PARTS * n)
    tiles = tile_pairs.shape[1]
    quarter = tiles // 4
    root_weight = jnp.sqrt(obs_weight)[:, None]
    listed = tile_pairs.reshape(-1)
    far_listed = lax.ppermute(listed, "part", [(0, 1), (1, 0)])
    smem = pl.BlockSpec(memory_space=pltpu.SMEM)
    vmem = pl.BlockSpec(memory_space=pltpu.VMEM)
    dma = pltpu.SemaphoreType.DMA
    here = lax.axis_index("part")
    orders = block_order.reshape(PARTS, -1)
    orders = jnp.where(here == 0, orders[::-1], orders).reshape(-1)
    sent = order_columns(jacobian, root_weight, orders, PARTS, n)
    held_cols = pltpu.VMEM((slots, n * rows, BLOCK), jnp.bfloat16)
    group = (quarter, BLOCK, BLOCK)
    held = pl.pallas_call(
        functools.partial(kernel, n, rows, quarter),
        out_shape=jax.ShapeDtypeStruct(group, jnp.float32),
        in_specs=[smem, smem, pl.BlockSpec(memory_space=pl.ANY)],
        out_specs=vmem,
        scratch_shapes=[
            held_cols,
            held_cols,
            pltpu.VMEM((4,) + group, jnp.float32),
            pltpu.VMEM((4,) + group, jnp.float32),
            pltpu.VMEM((2, 2) + group, jnp.float32),
            pltpu.VMEM((2,) + group, jnp.float32),
            pltpu.VMEM(group, jnp.float32),
            dma((n,)), dma((n,)), dma((n,)), dma((n,)),
            dma((2, 2)), dma((2, 2)), dma((2,)), dma((2,)), dma, dma,
        ],
        compiler_params=pltpu.CompilerParams(
            collective_id=0, has_side_effects=True, vmem_limit_bytes=56 << 20),
    )(listed, far_listed, sent)
    ids = lax.axis_index("tile") * quarter + jnp.arange(quarter, dtype=jnp.int32)
    return jnp.where((ids < tile_count)[:, None, None], held, 0.0)


def solution(mesh):
    owners, tile_size = mesh.devices.shape
    n = owners // PARTS
    split_mesh = Mesh(mesh.devices.reshape(PARTS, n, tile_size), ("part", "obs", "tile"))
    every = ("part", "obs", "tile")
    return jax.shard_map(
        functools.partial(body, n),
        mesh=split_mesh,
        in_specs=(P(every, None), P(every), P(), P(("part", "obs"), None, None), P(("part", "obs"))),
        out_specs=P(every, None, None),
        check_vma=False,
    )
```

```python
import functools
import jax
import jax.numpy as jnp
from jax import lax
from jax.experimental import pallas as pl
from jax.experimental.pallas import tpu as pltpu
from jax.sharding import Mesh, PartitionSpec as P

BLOCK = 128
PARTS = 2


def order_kernel(slots, parts, per_part, order_ref, jac_ref, weight_ref, out_ref):
    dest, part = pl.program_id(0), pl.program_id(1)
    first = (part * per_part + dest) * slots
    weight = jnp.broadcast_to(weight_ref[...], (weight_ref.shape[0], BLOCK))

    def one(slot, carry):
        start = pl.multiple_of(order_ref[first + slot] * BLOCK, BLOCK)
        piece = jac_ref[:, pl.ds(start, BLOCK)].astype(jnp.float32) * weight
        out_ref[0, 0, slot] = piece.astype(jnp.bfloat16)
        return carry

    lax.fori_loop(0, slots, one, 0, unroll=8)


def order_columns(jacobian, root_weight, block_order, parts, per_part):
    rows, width = jacobian.shape
    slots = block_order.shape[0] // (parts * per_part)
    return pl.pallas_call(
        functools.partial(order_kernel, slots, parts, per_part),
        out_shape=jax.ShapeDtypeStruct((per_part, parts, slots, rows, BLOCK), jnp.bfloat16),
        grid_spec=pltpu.PrefetchScalarGridSpec(
            num_scalar_prefetch=1,
            grid=(per_part, parts),
            in_specs=[
                pl.BlockSpec((rows, width), lambda d, p, order: (0, 0)),
                pl.BlockSpec((rows, 1), lambda d, p, order: (0, 0)),
            ],
            out_specs=pl.BlockSpec((1, 1, slots, rows, BLOCK), lambda d, p, order: (d, p, 0, 0, 0)),
        ),
        compiler_params=pltpu.CompilerParams(vmem_limit_bytes=48 << 20),
    )(block_order, jacobian, root_weight)


def kernel(n, rows, quarter, own_list, far_list, sent_ref, out_ref,
           far_cols, own_cols, far_tiles, own_tiles, pair_in, side_in, part_in,
           far_ss, far_rs, own_ss, own_rs, pair_ss, pair_rs, side_ss, side_rs, part_ss, part_rs):
    part, me, t = lax.axis_index("part"), lax.axis_index("obs"), lax.axis_index("tile")
    hi, lo = t // 2, t % 2
    pair_peer = {"tile": hi * 2 + (1 - lo)}
    side_peer = {"tile": (1 - hi) * 2 + lo}
    part_peer = {"part": 1 - part}
    peers = [{"obs": (me + d) % n} for d in range(n)]
    mesh_id = pl.DeviceIdType.MESH

    barrier = pltpu.get_barrier_semaphore()
    for peer in peers[1:] + [pair_peer, side_peer, part_peer]:
        pl.semaphore_signal(barrier, inc=1, device_id=peer, device_id_type=mesh_id)

    def send(source, target, ss, rs, peer):
        return pltpu.make_async_remote_copy(
            src_ref=source, dst_ref=target, send_sem=ss, recv_sem=rs,
            device_id=peer, device_id_type=mesh_id)

    far_moves, own_moves = [None], [None]
    for d in range(1, n):
        dest = (me + d) % n
        place = pl.ds(d * rows, rows)
        far_moves.append(
            send(sent_ref.at[dest, 0], far_cols.at[:, place], far_ss.at[d], far_rs.at[d], peers[d]))
        own_moves.append(
            send(sent_ref.at[dest, 1], own_cols.at[:, place], own_ss.at[d], own_rs.at[d], peers[d]))
    far_kept = pltpu.make_async_copy(sent_ref.at[me, 0], far_cols.at[:, pl.ds(0, rows)], far_ss.at[0])
    own_kept = pltpu.make_async_copy(sent_ref.at[me, 1], own_cols.at[:, pl.ds(0, rows)], own_ss.at[0])
    pl.semaphore_wait(barrier, n + 2)
    for d in range(1, n):
        far_moves[d].start()
    far_kept.start()
    own_kept.start()
    for d in range(1, n):
        far_moves[d].wait_send()
        own_moves[d].start()
    far_kept.wait()
    own_kept.wait()

    half = quarter // 2
    halves = [pl.ds(0, half), pl.ds(half, half)]

    def products(listed, columns, tiles, q, place, first, size):
        def one(i, carry):
            tile = q * quarter + first + i
            left = columns[listed[2 * tile]]
            right = columns[listed[2 * tile + 1]]
            tiles[place, first + i] = lax.dot_general(
                left, right, (((0,), (0,)), ((), ())), preferred_element_type=jnp.float32)
            return carry

        lax.fori_loop(0, size, one, 0, unroll=4)

    def reduce(phase, listed, columns, tiles):
        near, side = [], []
        for i, part_half in enumerate(halves):
            near.append(send(tiles.at[0, part_half], pair_in.at[phase, 0, part_half],
                             pair_ss.at[phase, i], pair_rs.at[phase, i], pair_peer))
            side.append(send(tiles.at[1, part_half], side_in.at[phase, part_half],
                             side_ss.at[phase, i], side_rs.at[phase, i], side_peer))
        near.append(send(tiles.at[2], pair_in.at[phase, 1],
                         pair_ss.at[phase, 2], pair_rs.at[phase, 2], pair_peer))
        for i, part_half in enumerate(halves):
            products(listed, columns, tiles, (1 - hi) * 2 + (1 - lo), 0, i * half, half)
            near[i].start()
            products(listed, columns, tiles, (1 - hi) * 2 + lo, 1, i * half, half)
            near[i].wait_recv()
            tiles[1, part_half] = tiles[1, part_half] + pair_in[phase, 0, part_half]
            side[i].start()
        products(listed, columns, tiles, hi * 2 + (1 - lo), 2, 0, quarter)
        near[2].start()
        products(listed, columns, tiles, hi * 2 + lo, 3, 0, quarter)
        near[2].wait_recv()
        tiles[3] = tiles[3] + pair_in[phase, 1]
        return near, side

    for d in range(1, n):
        far_moves[d].wait_recv()
    far_near, far_side = reduce(0, far_list, far_cols, far_tiles)
    for move in far_side:
        move.wait_recv()
    far_tiles[3] = far_tiles[3] + side_in[0]
    across = send(far_tiles.at[3], part_in, part_ss, part_rs, part_peer)
    across.start()
    for d in range(1, n):
        own_moves[d].wait_recv()
    own_near, own_side = reduce(1, own_list, own_cols, own_tiles)
    across.wait_recv()
    own_tiles[3] = own_tiles[3] + part_in[...]
    for move in own_side:
        move.wait_recv()
    out_ref[...] = own_tiles[3] + side_in[1]
    for d in range(1, n):
        own_moves[d].wait_send()
    for move in far_near + own_near + far_side + own_side + [across]:
        move.wait_send()


def body(n, jacobian, obs_weight, block_order, tile_pairs, tile_count):
    rows, width = jacobian.shape
    slots = block_order.shape[0] // (PARTS * n)
    tiles = tile_pairs.shape[1]
    quarter = tiles // 4
    root_weight = jnp.sqrt(obs_weight)[:, None]
    listed = tile_pairs.reshape(-1)
    far_listed = lax.ppermute(listed, "part", [(0, 1), (1, 0)])
    smem = pl.BlockSpec(memory_space=pltpu.SMEM)
    vmem = pl.BlockSpec(memory_space=pltpu.VMEM)
    dma = pltpu.SemaphoreType.DMA
    here = lax.axis_index("part")
    orders = block_order.reshape(PARTS, -1)
    orders = jnp.where(here == 0, orders[::-1], orders).reshape(-1)
    sent = order_columns(jacobian, root_weight, orders, PARTS, n)
    held_cols = pltpu.VMEM((slots, n * rows, BLOCK), jnp.bfloat16)
    group = (quarter, BLOCK, BLOCK)
    held = pl.pallas_call(
        functools.partial(kernel, n, rows, quarter),
        out_shape=jax.ShapeDtypeStruct(group, jnp.float32),
        in_specs=[smem, smem, pl.BlockSpec(memory_space=pl.ANY)],
        out_specs=vmem,
        scratch_shapes=[
            held_cols,
            held_cols,
            pltpu.VMEM((4,) + group, jnp.float32),
            pltpu.VMEM((4,) + group, jnp.float32),
            pltpu.VMEM((2, 2) + group, jnp.float32),
            pltpu.VMEM((2,) + group, jnp.float32),
            pltpu.VMEM(group, jnp.float32),
            dma((n,)), dma((n,)), dma((n,)), dma((n,)),
            dma((2, 3)), dma((2, 3)), dma((2, 2)), dma((2, 2)), dma, dma,
        ],
        compiler_params=pltpu.CompilerParams(
            collective_id=0, has_side_effects=True, vmem_limit_bytes=56 << 20),
    )(listed, far_listed, sent)
    ids = lax.axis_index("tile") * quarter + jnp.arange(quarter, dtype=jnp.int32)
    return jnp.where((ids < tile_count)[:, None, None], held, 0.0)


def solution(mesh):
    owners, tile_size = mesh.devices.shape
    n = owners // PARTS
    split_mesh = Mesh(mesh.devices.reshape(PARTS, n, tile_size), ("part", "obs", "tile"))
    every = ("part", "obs", "tile")
    return jax.shard_map(
        functools.partial(body, n),
        mesh=split_mesh,
        in_specs=(P(every, None), P(every), P(), P(("part", "obs"), None, None), P(("part", "obs"))),
        out_specs=P(every, None, None),
        check_vma=False,
    )
```

```python
import functools
import jax
import jax.numpy as jnp
from jax import lax
from jax.experimental import pallas as pl
from jax.experimental.pallas import tpu as pltpu
from jax.sharding import Mesh, PartitionSpec as P

BLOCK = 128
PARTS = 2


def order_kernel(slots, parts, per_part, order_ref, jac_ref, weight_ref, out_ref):
    dest = pl.program_id(0)
    weight = jnp.broadcast_to(weight_ref[...], (weight_ref.shape[0], BLOCK))

    for part in range(parts):
        first = (part * per_part + dest) * slots

        def one(slot, carry, part=part, first=first):
            start = pl.multiple_of(order_ref[first + slot] * BLOCK, BLOCK)
            piece = jac_ref[:, pl.ds(start, BLOCK)].astype(jnp.float32) * weight
            out_ref[0, part, slot] = piece.astype(jnp.bfloat16)
            return carry

        lax.fori_loop(0, slots, one, 0, unroll=8)


def order_columns(jacobian, root_weight, block_order, parts, per_part):
    rows, width = jacobian.shape
    slots = block_order.shape[0] // (parts * per_part)
    return pl.pallas_call(
        functools.partial(order_kernel, slots, parts, per_part),
        out_shape=jax.ShapeDtypeStruct((per_part, parts, slots, rows, BLOCK), jnp.bfloat16),
        grid_spec=pltpu.PrefetchScalarGridSpec(
            num_scalar_prefetch=1,
            grid=(per_part,),
            in_specs=[
                pl.BlockSpec((rows, width), lambda d, order: (0, 0)),
                pl.BlockSpec((rows, 1), lambda d, order: (0, 0)),
            ],
            out_specs=pl.BlockSpec((1, parts, slots, rows, BLOCK), lambda d, order: (d, 0, 0, 0, 0)),
        ),
        compiler_params=pltpu.CompilerParams(vmem_limit_bytes=48 << 20),
    )(block_order, jacobian, root_weight)


def kernel(n, rows, quarter, own_list, own_row, sent_ref, out_ref,
           far_row, far_list, far_cols, own_cols, far_tiles, own_tiles, pair_in, side_in, part_in,
           far_ss, far_rs, own_ss, own_rs, pair_ss, pair_rs, side_ss, side_rs, part_ss, part_rs, list_ss, list_rs):
    part, me, t = lax.axis_index("part"), lax.axis_index("obs"), lax.axis_index("tile")
    hi, lo = t // 2, t % 2
    pair_peer = {"tile": hi * 2 + (1 - lo)}
    side_peer = {"tile": (1 - hi) * 2 + lo}
    part_peer = {"part": 1 - part}
    peers = [{"obs": (me + d) % n} for d in range(n)]
    mesh_id = pl.DeviceIdType.MESH

    barrier = pltpu.get_barrier_semaphore()
    for peer in peers[1:] + [pair_peer, side_peer, part_peer]:
        pl.semaphore_signal(barrier, inc=1, device_id=peer, device_id_type=mesh_id)

    def send(source, target, ss, rs, peer):
        return pltpu.make_async_remote_copy(
            src_ref=source, dst_ref=target, send_sem=ss, recv_sem=rs,
            device_id=peer, device_id_type=mesh_id)

    far_moves, own_moves = [None], [None]
    for d in range(1, n):
        dest = (me + d) % n
        place = pl.ds(d * rows, rows)
        far_moves.append(
            send(sent_ref.at[dest, 0], far_cols.at[:, place], far_ss.at[d], far_rs.at[d], peers[d]))
        own_moves.append(
            send(sent_ref.at[dest, 1], own_cols.at[:, place], own_ss.at[d], own_rs.at[d], peers[d]))
    far_kept = pltpu.make_async_copy(sent_ref.at[me, 0], far_cols.at[:, pl.ds(0, rows)], far_ss.at[0])
    own_kept = pltpu.make_async_copy(sent_ref.at[me, 1], own_cols.at[:, pl.ds(0, rows)], own_ss.at[0])
    pl.semaphore_wait(barrier, n + 2)
    for d in range(1, n):
        far_moves[d].start()
    list_move = send(own_row, far_row, list_ss.at[0], list_rs, part_peer)
    list_move.start()
    far_kept.start()
    own_kept.start()
    for d in range(1, n):
        far_moves[d].wait_send()
        own_moves[d].start()
    far_kept.wait()
    own_kept.wait()
    list_move.wait()
    list_kept = pltpu.make_async_copy(far_row, far_list, list_ss.at[1])
    list_kept.start()
    list_kept.wait()

    half = quarter // 2
    halves = [pl.ds(0, half), pl.ds(half, half)]

    def products(listed, columns, tiles, q, place, first, size):
        def one(i, carry):
            tile = q * quarter + first + i
            left = columns[listed[0, 2 * tile]]
            right = columns[listed[0, 2 * tile + 1]]
            tiles[place, first + i] = lax.dot_general(
                left, right, (((0,), (0,)), ((), ())), preferred_element_type=jnp.float32)
            return carry

        lax.fori_loop(0, size, one, 0, unroll=4)

    def reduce(phase, listed, columns, tiles):
        near, side = [], []
        for i, part_half in enumerate(halves):
            near.append(send(tiles.at[0, part_half], pair_in.at[phase, 0, part_half],
                             pair_ss.at[phase, i], pair_rs.at[phase, i], pair_peer))
            side.append(send(tiles.at[1, part_half], side_in.at[phase, part_half],
                             side_ss.at[phase, i], side_rs.at[phase, i], side_peer))
        near.append(send(tiles.at[2], pair_in.at[phase, 1],
                         pair_ss.at[phase, 2], pair_rs.at[phase, 2], pair_peer))
        for i, part_half in enumerate(halves):
            products(listed, columns, tiles, (1 - hi) * 2 + (1 - lo), 0, i * half, half)
            near[i].start()
            products(listed, columns, tiles, (1 - hi) * 2 + lo, 1, i * half, half)
            near[i].wait_recv()
            tiles[1, part_half] = tiles[1, part_half] + pair_in[phase, 0, part_half]
            side[i].start()
        products(listed, columns, tiles, hi * 2 + (1 - lo), 2, 0, quarter)
        near[2].start()
        products(listed, columns, tiles, hi * 2 + lo, 3, 0, quarter)
        near[2].wait_recv()
        tiles[3] = tiles[3] + pair_in[phase, 1]
        return near, side

    for d in range(1, n):
        far_moves[d].wait_recv()
    far_near, far_side = reduce(0, far_list, far_cols, far_tiles)
    across = []
    for i, part_half in enumerate(halves):
        far_side[i].wait_recv()
        far_tiles[3, part_half] = far_tiles[3, part_half] + side_in[0, part_half]
        across.append(send(far_tiles.at[3, part_half], part_in.at[part_half],
                           part_ss.at[i], part_rs.at[i], part_peer))
        across[i].start()
    for d in range(1, n):
        own_moves[d].wait_recv()
    own_near, own_side = reduce(1, own_list, own_cols, own_tiles)
    for i, part_half in enumerate(halves):
        across[i].wait_recv()
        own_side[i].wait_recv()
        out_ref[part_half] = (own_tiles[3, part_half] + part_in[part_half]) + side_in[1, part_half]
    for d in range(1, n):
        own_moves[d].wait_send()
    for move in far_near + own_near + far_side + own_side + across:
        move.wait_send()


def body(n, jacobian, obs_weight, block_order, tile_pairs, tile_count):
    rows, width = jacobian.shape
    slots = block_order.shape[0] // (PARTS * n)
    tiles = tile_pairs.shape[1]
    quarter = tiles // 4
    root_weight = jnp.sqrt(obs_weight)[:, None]
    listed = tile_pairs.reshape(1, -1)
    smem = pl.BlockSpec(memory_space=pltpu.SMEM)
    vmem = pl.BlockSpec(memory_space=pltpu.VMEM)
    dma = pltpu.SemaphoreType.DMA
    here = lax.axis_index("part")
    orders = block_order.reshape(PARTS, -1)
    orders = jnp.where(here == 0, orders[::-1], orders).reshape(-1)
    sent = order_columns(jacobian, root_weight, orders, PARTS, n)
    held_cols = pltpu.VMEM((slots, n * rows, BLOCK), jnp.bfloat16)
    group = (quarter, BLOCK, BLOCK)
    held = pl.pallas_call(
        functools.partial(kernel, n, rows, quarter),
        out_shape=jax.ShapeDtypeStruct(group, jnp.float32),
        in_specs=[smem, vmem, pl.BlockSpec(memory_space=pl.ANY)],
        out_specs=vmem,
        scratch_shapes=[
            pltpu.VMEM(listed.shape, jnp.int32),
            pltpu.SMEM(listed.shape, jnp.int32),
            held_cols,
            held_cols,
            pltpu.VMEM((4,) + group, jnp.float32),
            pltpu.VMEM((4,) + group, jnp.float32),
            pltpu.VMEM((2, 2) + group, jnp.float32),
            pltpu.VMEM((2,) + group, jnp.float32),
            pltpu.VMEM(group, jnp.float32),
            dma((n,)), dma((n,)), dma((n,)), dma((n,)),
            dma((2, 3)), dma((2, 3)), dma((2, 2)), dma((2, 2)), dma((2,)), dma((2,)), dma((2,)), dma,
        ],
        compiler_params=pltpu.CompilerParams(
            collective_id=0, has_side_effects=True, vmem_limit_bytes=56 << 20),
    )(listed, listed, sent)
    ids = lax.axis_index("tile") * quarter + jnp.arange(quarter, dtype=jnp.int32)
    return jnp.where((ids < tile_count)[:, None, None], held, 0.0)


def solution(mesh):
    owners, tile_size = mesh.devices.shape
    n = owners // PARTS
    split_mesh = Mesh(mesh.devices.reshape(PARTS, n, tile_size), ("part", "obs", "tile"))
    every = ("part", "obs", "tile")
    return jax.shard_map(
        functools.partial(body, n),
        mesh=split_mesh,
        in_specs=(P(every, None), P(every), P(), P(("part", "obs"), None, None), P(("part", "obs"))),
        out_specs=P(every, None, None),
        check_vma=False,
    )
```

```python
import functools
import jax
import jax.numpy as jnp
from jax import lax
from jax.experimental import pallas as pl
from jax.experimental.pallas import tpu as pltpu
from jax.sharding import Mesh, PartitionSpec as P

BLOCK = 128
PARTS = 2


def order_kernel(slots, parts, per_part, order_ref, jac_ref, weight_ref, out_ref):
    dest = pl.program_id(0)
    weight = jnp.broadcast_to(weight_ref[...], (weight_ref.shape[0], BLOCK))

    for part in range(parts):
        first = (part * per_part + dest) * slots

        def one(slot, carry, part=part, first=first):
            start = pl.multiple_of(order_ref[first + slot] * BLOCK, BLOCK)
            piece = jac_ref[:, pl.ds(start, BLOCK)].astype(jnp.float32) * weight
            out_ref[0, part, slot] = piece.astype(jnp.bfloat16)
            return carry

        lax.fori_loop(0, slots, one, 0, unroll=8)


def order_columns(jacobian, root_weight, block_order, parts, per_part):
    rows, width = jacobian.shape
    slots = block_order.shape[0] // (parts * per_part)
    return pl.pallas_call(
        functools.partial(order_kernel, slots, parts, per_part),
        out_shape=jax.ShapeDtypeStruct((per_part, parts, slots, rows, BLOCK), jnp.bfloat16),
        grid_spec=pltpu.PrefetchScalarGridSpec(
            num_scalar_prefetch=1,
            grid=(per_part,),
            in_specs=[
                pl.BlockSpec((rows, width), lambda d, order: (0, 0)),
                pl.BlockSpec((rows, 1), lambda d, order: (0, 0)),
            ],
            out_specs=pl.BlockSpec((1, parts, slots, rows, BLOCK), lambda d, order: (d, 0, 0, 0, 0)),
        ),
        compiler_params=pltpu.CompilerParams(vmem_limit_bytes=48 << 20),
    )(block_order, jacobian, root_weight)


def partner(n, me, d):
    other, bit = 0, 1
    while bit < n:
        other = other + (me // bit + d // bit) % 2 * bit
        bit *= 2
    return other


def kernel(n, rows, quarter, own_list, own_row, sent_ref, out_ref,
           far_row, far_list, far_cols, own_cols, far_tiles, own_tiles, pair_in, side_in, part_in,
           far_ss, far_rs, own_ss, own_rs, pair_ss, pair_rs, side_ss, side_rs, part_ss, part_rs, list_ss, list_rs):
    part, me, t = lax.axis_index("part"), lax.axis_index("obs"), lax.axis_index("tile")
    hi, lo = t // 2, t % 2
    pair_peer = {"tile": hi * 2 + (1 - lo)}
    side_peer = {"tile": (1 - hi) * 2 + lo}
    part_peer = {"part": 1 - part}
    peers = [{"obs": partner(n, me, d)} for d in range(n)]
    mesh_id = pl.DeviceIdType.MESH

    barrier = pltpu.get_barrier_semaphore()
    for peer in peers[1:] + [pair_peer, side_peer, part_peer]:
        pl.semaphore_signal(barrier, inc=1, device_id=peer, device_id_type=mesh_id)

    def send(source, target, ss, rs, peer):
        return pltpu.make_async_remote_copy(
            src_ref=source, dst_ref=target, send_sem=ss, recv_sem=rs,
            device_id=peer, device_id_type=mesh_id)

    far_moves, own_moves = [None], [None]
    for d in range(1, n):
        dest = partner(n, me, d)
        place = pl.ds(d * rows, rows)
        far_moves.append(
            send(sent_ref.at[dest, 0], far_cols.at[:, place], far_ss.at[d], far_rs.at[d], peers[d]))
        own_moves.append(
            send(sent_ref.at[dest, 1], own_cols.at[:, place], own_ss.at[d], own_rs.at[d], peers[d]))
    far_kept = pltpu.make_async_copy(sent_ref.at[me, 0], far_cols.at[:, pl.ds(0, rows)], far_ss.at[0])
    own_kept = pltpu.make_async_copy(sent_ref.at[me, 1], own_cols.at[:, pl.ds(0, rows)], own_ss.at[0])
    pl.semaphore_wait(barrier, n + 2)
    for d in reversed(range(1, n)):
        far_moves[d].start()
    list_move = send(own_row, far_row, list_ss.at[0], list_rs, part_peer)
    list_move.start()
    far_kept.start()
    own_kept.start()
    for d in reversed(range(1, n)):
        far_moves[d].wait_send()
        own_moves[d].start()
    far_kept.wait()
    own_kept.wait()
    list_move.wait()
    list_kept = pltpu.make_async_copy(far_row, far_list, list_ss.at[1])
    list_kept.start()
    list_kept.wait()

    half = quarter // 2
    halves = [pl.ds(0, half), pl.ds(half, half)]

    def products(listed, columns, tiles, q, place, first, size):
        def one(i, carry):
            tile = q * quarter + first + i
            left = columns[listed[0, 2 * tile]]
            right = columns[listed[0, 2 * tile + 1]]
            tiles[place, first + i] = lax.dot_general(
                left, right, (((0,), (0,)), ((), ())), preferred_element_type=jnp.float32)
            return carry

        lax.fori_loop(0, size, one, 0, unroll=4)

    def reduce(phase, listed, columns, tiles):
        near, side = [], []
        for i, part_half in enumerate(halves):
            near.append(send(tiles.at[0, part_half], pair_in.at[phase, 0, part_half],
                             pair_ss.at[phase, i], pair_rs.at[phase, i], pair_peer))
            side.append(send(tiles.at[1, part_half], side_in.at[phase, part_half],
                             side_ss.at[phase, i], side_rs.at[phase, i], side_peer))
        near.append(send(tiles.at[2], pair_in.at[phase, 1],
                         pair_ss.at[phase, 2], pair_rs.at[phase, 2], pair_peer))
        for i, part_half in enumerate(halves):
            products(listed, columns, tiles, (1 - hi) * 2 + (1 - lo), 0, i * half, half)
            near[i].start()
            products(listed, columns, tiles, (1 - hi) * 2 + lo, 1, i * half, half)
            near[i].wait_recv()
            tiles[1, part_half] = tiles[1, part_half] + pair_in[phase, 0, part_half]
            side[i].start()
        products(listed, columns, tiles, hi * 2 + (1 - lo), 2, 0, quarter)
        near[2].start()
        products(listed, columns, tiles, hi * 2 + lo, 3, 0, quarter)
        near[2].wait_recv()
        tiles[3] = tiles[3] + pair_in[phase, 1]
        return near, side

    for d in range(1, n):
        far_moves[d].wait_recv()
    far_near, far_side = reduce(0, far_list, far_cols, far_tiles)
    for move in far_side:
        move.wait_recv()
    far_tiles[3] = far_tiles[3] + side_in[0]
    across = send(far_tiles.at[3], part_in, part_ss, part_rs, part_peer)
    across.start()
    for d in range(1, n):
        own_moves[d].wait_recv()
    own_near, own_side = reduce(1, own_list, own_cols, own_tiles)
    across.wait_recv()
    for i, part_half in enumerate(halves):
        own_side[i].wait_recv()
        out_ref[part_half] = (own_tiles[3, part_half] + part_in[part_half]) + side_in[1, part_half]
    for d in range(1, n):
        own_moves[d].wait_send()
    for move in far_near + own_near + far_side + own_side + [across]:
        move.wait_send()


def body(n, jacobian, obs_weight, block_order, tile_pairs, tile_count):
    rows, width = jacobian.shape
    slots = block_order.shape[0] // (PARTS * n)
    tiles = tile_pairs.shape[1]
    quarter = tiles // 4
    root_weight = jnp.sqrt(obs_weight)[:, None]
    listed = tile_pairs.reshape(1, -1)
    smem = pl.BlockSpec(memory_space=pltpu.SMEM)
    vmem = pl.BlockSpec(memory_space=pltpu.VMEM)
    dma = pltpu.SemaphoreType.DMA
    here = lax.axis_index("part")
    orders = block_order.reshape(PARTS, -1)
    orders = jnp.where(here == 0, orders[::-1], orders).reshape(-1)
    sent = order_columns(jacobian, root_weight, orders, PARTS, n)
    held_cols = pltpu.VMEM((slots, n * rows, BLOCK), jnp.bfloat16)
    group = (quarter, BLOCK, BLOCK)
    held = pl.pallas_call(
        functools.partial(kernel, n, rows, quarter),
        out_shape=jax.ShapeDtypeStruct(group, jnp.float32),
        in_specs=[smem, vmem, pl.BlockSpec(memory_space=pl.ANY)],
        out_specs=vmem,
        scratch_shapes=[
            pltpu.VMEM(listed.shape, jnp.int32),
            pltpu.SMEM(listed.shape, jnp.int32),
            held_cols,
            held_cols,
            pltpu.VMEM((4,) + group, jnp.float32),
            pltpu.VMEM((4,) + group, jnp.float32),
            pltpu.VMEM((2, 2) + group, jnp.float32),
            pltpu.VMEM((2,) + group, jnp.float32),
            pltpu.VMEM(group, jnp.float32),
            dma((n,)), dma((n,)), dma((n,)), dma((n,)),
            dma((2, 3)), dma((2, 3)), dma((2, 2)), dma((2, 2)), dma, dma, dma((2,)), dma,
        ],
        compiler_params=pltpu.CompilerParams(
            collective_id=0, has_side_effects=True, vmem_limit_bytes=56 << 20),
    )(listed, listed, sent)
    ids = lax.axis_index("tile") * quarter + jnp.arange(quarter, dtype=jnp.int32)
    return jnp.where((ids < tile_count)[:, None, None], held, 0.0)


def solution(mesh):
    owners, tile_size = mesh.devices.shape
    n = owners // PARTS
    assert n & (n - 1) == 0 and tile_size == 4
    split_mesh = Mesh(mesh.devices.reshape(PARTS, n, tile_size), ("part", "obs", "tile"))
    every = ("part", "obs", "tile")
    return jax.shard_map(
        functools.partial(body, n),
        mesh=split_mesh,
        in_specs=(P(every, None), P(every), P(), P(("part", "obs"), None, None), P(("part", "obs"))),
        out_specs=P(every, None, None),
        check_vma=False,
    )
```

```python
import functools
import jax
import jax.numpy as jnp
from jax import lax
from jax.experimental import pallas as pl
from jax.experimental.pallas import tpu as pltpu
from jax.sharding import Mesh, PartitionSpec as P

BLOCK = 128
PARTS = 2


def order_kernel(slots, parts, per_part, order_ref, jac_ref, weight_ref, out_ref):
    dest = pl.program_id(0)
    weight = jnp.broadcast_to(weight_ref[...], (weight_ref.shape[0], BLOCK))

    for part in range(parts):
        first = (part * per_part + dest) * slots

        def one(slot, carry, part=part, first=first):
            start = pl.multiple_of(order_ref[first + slot] * BLOCK, BLOCK)
            piece = jac_ref[:, pl.ds(start, BLOCK)].astype(jnp.float32) * weight
            out_ref[0, part, slot] = piece.astype(jnp.bfloat16)
            return carry

        lax.fori_loop(0, slots, one, 0, unroll=8)


def order_columns(jacobian, root_weight, block_order, parts, per_part):
    rows, width = jacobian.shape
    slots = block_order.shape[0] // (parts * per_part)
    return pl.pallas_call(
        functools.partial(order_kernel, slots, parts, per_part),
        out_shape=jax.ShapeDtypeStruct((per_part, parts, slots, rows, BLOCK), jnp.bfloat16),
        grid_spec=pltpu.PrefetchScalarGridSpec(
            num_scalar_prefetch=1,
            grid=(per_part,),
            in_specs=[
                pl.BlockSpec((rows, width), lambda d, order: (0, 0)),
                pl.BlockSpec((rows, 1), lambda d, order: (0, 0)),
            ],
            out_specs=pl.BlockSpec((1, parts, slots, rows, BLOCK), lambda d, order: (d, 0, 0, 0, 0)),
        ),
        compiler_params=pltpu.CompilerParams(vmem_limit_bytes=48 << 20),
    )(block_order, jacobian, root_weight)


def partner(n, me, d):
    other, bit = 0, 1
    while bit < n:
        other = other + (me // bit + d // bit) % 2 * bit
        bit *= 2
    return other


def kernel(n, rows, quarter, own_list, own_row, sent_ref, out_ref,
           far_row, far_list, far_cols, own_cols, far_tiles, own_tiles, pair_in, side_in, part_in,
           far_ss, far_rs, own_ss, own_rs, pair_ss, pair_rs, side_ss, side_rs, part_ss, part_rs, list_ss, list_rs):
    part, me, t = lax.axis_index("part"), lax.axis_index("obs"), lax.axis_index("tile")
    hi, lo = t // 2, t % 2
    pair_peer = {"tile": hi * 2 + (1 - lo)}
    side_peer = {"tile": (1 - hi) * 2 + lo}
    part_peer = {"part": 1 - part}
    peers = [{"obs": partner(n, me, d)} for d in range(n)]
    mesh_id = pl.DeviceIdType.MESH

    barrier = pltpu.get_barrier_semaphore()
    for peer in peers[1:] + [pair_peer, side_peer, part_peer]:
        pl.semaphore_signal(barrier, inc=1, device_id=peer, device_id_type=mesh_id)

    def send(source, target, ss, rs, peer):
        return pltpu.make_async_remote_copy(
            src_ref=source, dst_ref=target, send_sem=ss, recv_sem=rs,
            device_id=peer, device_id_type=mesh_id)

    far_moves, own_moves = [None], [None]
    for d in range(1, n):
        dest = partner(n, me, d)
        place = pl.ds(d * rows, rows)
        far_moves.append(
            send(sent_ref.at[dest, 0], far_cols.at[:, place], far_ss.at[d], far_rs.at[d], peers[d]))
        own_moves.append(
            send(sent_ref.at[dest, 1], own_cols.at[:, place], own_ss.at[d], own_rs.at[d], peers[d]))
    far_kept = pltpu.make_async_copy(sent_ref.at[me, 0], far_cols.at[:, pl.ds(0, rows)], far_ss.at[0])
    own_kept = pltpu.make_async_copy(sent_ref.at[me, 1], own_cols.at[:, pl.ds(0, rows)], own_ss.at[0])
    pl.semaphore_wait(barrier, n + 2)
    for d in reversed(range(1, n)):
        far_moves[d].start()
    list_move = send(own_row, far_row, list_ss.at[0], list_rs, part_peer)
    list_move.start()
    far_kept.start()
    own_kept.start()
    for d in reversed(range(1, n)):
        far_moves[d].wait_send()
        own_moves[d].start()
    far_kept.wait()
    own_kept.wait()
    list_move.wait()
    list_kept = pltpu.make_async_copy(far_row, far_list, list_ss.at[1])
    list_kept.start()
    list_kept.wait()

    half = quarter // 2
    halves = [pl.ds(0, half), pl.ds(half, half)]

    def products(listed, columns, tiles, q, place, first, size):
        def one(i, carry):
            tile = q * quarter + first + i
            left = columns[listed[0, 2 * tile]]
            right = columns[listed[0, 2 * tile + 1]]
            tiles[place, first + i] = lax.dot_general(
                left, right, (((0,), (0,)), ((), ())), preferred_element_type=jnp.float32)
            return carry

        lax.fori_loop(0, size, one, 0, unroll=4)

    def reduce(phase, listed, columns, tiles):
        near, side = [], []
        for i, part_half in enumerate(halves):
            near.append(send(tiles.at[0, part_half], pair_in.at[phase, 0, part_half],
                             pair_ss.at[phase, i], pair_rs.at[phase, i], pair_peer))
            side.append(send(tiles.at[1, part_half], side_in.at[phase, part_half],
                             side_ss.at[phase, i], side_rs.at[phase, i], side_peer))
        near.append(send(tiles.at[2], pair_in.at[phase, 1],
                         pair_ss.at[phase, 2], pair_rs.at[phase, 2], pair_peer))
        for i, part_half in enumerate(halves):
            products(listed, columns, tiles, (1 - hi) * 2 + (1 - lo), 0, i * half, half)
            near[i].start()
            products(listed, columns, tiles, (1 - hi) * 2 + lo, 1, i * half, half)
            near[i].wait_recv()
            tiles[1, part_half] = tiles[1, part_half] + pair_in[phase, 0, part_half]
            side[i].start()
        products(listed, columns, tiles, hi * 2 + (1 - lo), 2, 0, quarter)
        near[2].start()
        products(listed, columns, tiles, hi * 2 + lo, 3, 0, quarter)
        near[2].wait_recv()
        tiles[3] = tiles[3] + pair_in[phase, 1]
        return near, side

    for d in range(1, n):
        far_moves[d].wait_recv()
    far_near, far_side = reduce(0, far_list, far_cols, far_tiles)
    for move in far_side:
        move.wait_recv()
    far_tiles[3] = far_tiles[3] + side_in[0]
    early = quarter * 3 // 8
    across = [send(far_tiles.at[3, cut], part_in.at[cut], part_ss.at[i], part_rs.at[i], part_peer)
              for i, cut in enumerate([pl.ds(0, early), pl.ds(early, quarter - early)])]
    across[0].start()
    for d in range(1, n):
        own_moves[d].wait_recv()
    across[1].start()
    own_near, own_side = reduce(1, own_list, own_cols, own_tiles)
    for move in across:
        move.wait_recv()
    for i, part_half in enumerate(halves):
        own_side[i].wait_recv()
        out_ref[part_half] = (own_tiles[3, part_half] + part_in[part_half]) + side_in[1, part_half]
    for d in range(1, n):
        own_moves[d].wait_send()
    for move in far_near + own_near + far_side + own_side + across:
        move.wait_send()


def body(n, jacobian, obs_weight, block_order, tile_pairs, tile_count):
    rows, width = jacobian.shape
    slots = block_order.shape[0] // (PARTS * n)
    tiles = tile_pairs.shape[1]
    quarter = tiles // 4
    root_weight = jnp.sqrt(obs_weight)[:, None]
    listed = tile_pairs.reshape(1, -1)
    smem = pl.BlockSpec(memory_space=pltpu.SMEM)
    vmem = pl.BlockSpec(memory_space=pltpu.VMEM)
    dma = pltpu.SemaphoreType.DMA
    here = lax.axis_index("part")
    orders = block_order.reshape(PARTS, -1)
    orders = jnp.where(here == 0, orders[::-1], orders).reshape(-1)
    sent = order_columns(jacobian, root_weight, orders, PARTS, n)
    held_cols = pltpu.VMEM((slots, n * rows, BLOCK), jnp.bfloat16)
    group = (quarter, BLOCK, BLOCK)
    held = pl.pallas_call(
        functools.partial(kernel, n, rows, quarter),
        out_shape=jax.ShapeDtypeStruct(group, jnp.float32),
        in_specs=[smem, vmem, pl.BlockSpec(memory_space=pl.ANY)],
        out_specs=vmem,
        scratch_shapes=[
            pltpu.VMEM(listed.shape, jnp.int32),
            pltpu.SMEM(listed.shape, jnp.int32),
            held_cols,
            held_cols,
            pltpu.VMEM((4,) + group, jnp.float32),
            pltpu.VMEM((4,) + group, jnp.float32),
            pltpu.VMEM((2, 2) + group, jnp.float32),
            pltpu.VMEM((2,) + group, jnp.float32),
            pltpu.VMEM(group, jnp.float32),
            dma((n,)), dma((n,)), dma((n,)), dma((n,)),
            dma((2, 3)), dma((2, 3)), dma((2, 2)), dma((2, 2)), dma((2,)), dma((2,)), dma((2,)), dma,
        ],
        compiler_params=pltpu.CompilerParams(
            collective_id=0, has_side_effects=True, vmem_limit_bytes=56 << 20),
    )(listed, listed, sent)
    ids = lax.axis_index("tile") * quarter + jnp.arange(quarter, dtype=jnp.int32)
    return jnp.where((ids < tile_count)[:, None, None], held, 0.0)


def solution(mesh):
    owners, tile_size = mesh.devices.shape
    n = owners // PARTS
    assert n & (n - 1) == 0 and tile_size == 4
    split_mesh = Mesh(mesh.devices.reshape(PARTS, n, tile_size), ("part", "obs", "tile"))
    every = ("part", "obs", "tile")
    return jax.shard_map(
        functools.partial(body, n),
        mesh=split_mesh,
        in_specs=(P(every, None), P(every), P(), P(("part", "obs"), None, None), P(("part", "obs"))),
        out_specs=P(every, None, None),
        check_vma=False,
    )
```

```python
import functools
import jax
import jax.numpy as jnp
from jax import lax
from jax.experimental import pallas as pl
from jax.experimental.pallas import tpu as pltpu
from jax.sharding import Mesh, PartitionSpec as P

BLOCK = 128
PARTS = 2


def order_kernel(slots, parts, per_part, order_ref, jac_ref, weight_ref, out_ref):
    dest = pl.program_id(0)
    weight = jnp.broadcast_to(weight_ref[...], (weight_ref.shape[0], BLOCK))

    here = lax.axis_index("part")
    for part, owner_part in enumerate((1 - here, here)):
        first = (owner_part * per_part + dest) * slots

        def one(slot, carry, part=part, first=first):
            start = pl.multiple_of(order_ref[first + slot] * BLOCK, BLOCK)
            piece = jac_ref[:, pl.ds(start, BLOCK)].astype(jnp.float32) * weight
            out_ref[0, part, slot] = piece.astype(jnp.bfloat16)
            return carry

        lax.fori_loop(0, slots, one, 0, unroll=8)


def order_columns(jacobian, root_weight, block_order, parts, per_part):
    rows, width = jacobian.shape
    slots = block_order.shape[0] // (parts * per_part)
    return pl.pallas_call(
        functools.partial(order_kernel, slots, parts, per_part),
        out_shape=jax.ShapeDtypeStruct((per_part, parts, slots, rows, BLOCK), jnp.bfloat16),
        grid_spec=pltpu.PrefetchScalarGridSpec(
            num_scalar_prefetch=1,
            grid=(per_part,),
            in_specs=[
                pl.BlockSpec((rows, width), lambda d, order: (0, 0)),
                pl.BlockSpec((rows, 1), lambda d, order: (0, 0)),
            ],
            out_specs=pl.BlockSpec((1, parts, slots, rows, BLOCK), lambda d, order: (d, 0, 0, 0, 0)),
        ),
        compiler_params=pltpu.CompilerParams(vmem_limit_bytes=48 << 20),
    )(block_order, jacobian, root_weight)


def partner(n, me, d):
    other, bit = 0, 1
    while bit < n:
        other = other + (me // bit + d // bit) % 2 * bit
        bit *= 2
    return other


def kernel(n, rows, quarter, own_list, own_row, sent_ref, out_ref,
           far_row, far_list, far_cols, own_cols, far_tiles, own_tiles, pair_in, side_in, part_in,
           far_ss, far_rs, own_ss, own_rs, pair_ss, pair_rs, side_ss, side_rs, part_ss, part_rs, list_ss, list_rs):
    part, me, t = lax.axis_index("part"), lax.axis_index("obs"), lax.axis_index("tile")
    hi, lo = t // 2, t % 2
    pair_peer = {"tile": hi * 2 + (1 - lo)}
    side_peer = {"tile": (1 - hi) * 2 + lo}
    part_peer = {"part": 1 - part}
    peers = [{"obs": partner(n, me, d)} for d in range(n)]
    mesh_id = pl.DeviceIdType.MESH

    barrier = pltpu.get_barrier_semaphore()
    for peer in peers[1:] + [pair_peer, side_peer, part_peer]:
        pl.semaphore_signal(barrier, inc=1, device_id=peer, device_id_type=mesh_id)

    def send(source, target, ss, rs, peer):
        return pltpu.make_async_remote_copy(
            src_ref=source, dst_ref=target, send_sem=ss, recv_sem=rs,
            device_id=peer, device_id_type=mesh_id)

    far_moves, own_moves = [None], [None]
    for d in range(1, n):
        dest = partner(n, me, d)
        place = pl.ds(d * rows, rows)
        far_moves.append(
            send(sent_ref.at[dest, 0], far_cols.at[:, place], far_ss.at[d], far_rs.at[d], peers[d]))
        own_moves.append(
            send(sent_ref.at[dest, 1], own_cols.at[:, place], own_ss.at[d], own_rs.at[d], peers[d]))
    far_kept = pltpu.make_async_copy(sent_ref.at[me, 0], far_cols.at[:, pl.ds(0, rows)], far_ss.at[0])
    own_kept = pltpu.make_async_copy(sent_ref.at[me, 1], own_cols.at[:, pl.ds(0, rows)], own_ss.at[0])
    pl.semaphore_wait(barrier, n + 2)
    for d in reversed(range(1, n)):
        far_moves[d].start()
    list_move = send(own_row, far_row, list_ss.at[0], list_rs, part_peer)
    list_move.start()
    far_kept.start()
    own_kept.start()
    for d in reversed(range(1, n)):
        far_moves[d].wait_send()
        own_moves[d].start()
    far_kept.wait()
    own_kept.wait()
    list_move.wait()
    list_kept = pltpu.make_async_copy(far_row, far_list, list_ss.at[1])
    list_kept.start()
    list_kept.wait()

    half = quarter // 2
    halves = [pl.ds(0, half), pl.ds(half, half)]

    def products(listed, columns, tiles, q, place, first, size):
        def one(i, carry):
            tile = q * quarter + first + i
            left = columns[listed[0, 2 * tile]]
            right = columns[listed[0, 2 * tile + 1]]
            tiles[place, first + i] = lax.dot_general(
                left, right, (((0,), (0,)), ((), ())), preferred_element_type=jnp.float32)
            return carry

        lax.fori_loop(0, size, one, 0, unroll=8)

    def reduce(phase, listed, columns, tiles):
        near, side = [], []
        for i, part_half in enumerate(halves):
            near.append(send(tiles.at[0, part_half], pair_in.at[phase, 0, part_half],
                             pair_ss.at[phase, i], pair_rs.at[phase, i], pair_peer))
            side.append(send(tiles.at[1, part_half], side_in.at[phase, part_half],
                             side_ss.at[phase, i], side_rs.at[phase, i], side_peer))
        near.append(send(tiles.at[2], pair_in.at[phase, 1],
                         pair_ss.at[phase, 2], pair_rs.at[phase, 2], pair_peer))
        for i, part_half in enumerate(halves):
            products(listed, columns, tiles, (1 - hi) * 2 + (1 - lo), 0, i * half, half)
            near[i].start()
            products(listed, columns, tiles, (1 - hi) * 2 + lo, 1, i * half, half)
            near[i].wait_recv()
            tiles[1, part_half] = tiles[1, part_half] + pair_in[phase, 0, part_half]
            side[i].start()
        products(listed, columns, tiles, hi * 2 + (1 - lo), 2, 0, quarter)
        near[2].start()
        products(listed, columns, tiles, hi * 2 + lo, 3, 0, quarter)
        near[2].wait_recv()
        tiles[3] = tiles[3] + pair_in[phase, 1]
        return near, side

    for d in range(1, n):
        far_moves[d].wait_recv()
    far_near, far_side = reduce(0, far_list, far_cols, far_tiles)
    for move in far_side:
        move.wait_recv()
    far_tiles[3] = far_tiles[3] + side_in[0]
    early = quarter // 2
    across = [send(far_tiles.at[3, cut], part_in.at[cut], part_ss.at[i], part_rs.at[i], part_peer)
              for i, cut in enumerate([pl.ds(0, early), pl.ds(early, quarter - early)])]
    across[0].start()
    for d in range(1, n):
        own_moves[d].wait_recv()
    across[1].start()
    own_near, own_side = reduce(1, own_list, own_cols, own_tiles)
    for move in across:
        move.wait_recv()
    for i, part_half in enumerate(halves):
        own_side[i].wait_recv()
        out_ref[part_half] = (own_tiles[3, part_half] + part_in[part_half]) + side_in[1, part_half]
    for d in range(1, n):
        own_moves[d].wait_send()
    for move in far_near + own_near + far_side + own_side + across:
        move.wait_send()


def body(n, jacobian, obs_weight, block_order, tile_pairs, tile_count):
    rows, width = jacobian.shape
    slots = block_order.shape[0] // (PARTS * n)
    tiles = tile_pairs.shape[1]
    quarter = tiles // 4
    root_weight = jnp.sqrt(obs_weight)[:, None]
    listed = tile_pairs.reshape(1, -1)
    smem = pl.BlockSpec(memory_space=pltpu.SMEM)
    vmem = pl.BlockSpec(memory_space=pltpu.VMEM)
    dma = pltpu.SemaphoreType.DMA
    sent = order_columns(jacobian, root_weight, block_order, PARTS, n)
    held_cols = pltpu.VMEM((slots, n * rows, BLOCK), jnp.bfloat16)
    group = (quarter, BLOCK, BLOCK)
    held = pl.pallas_call(
        functools.partial(kernel, n, rows, quarter),
        out_shape=jax.ShapeDtypeStruct(group, jnp.float32),
        in_specs=[smem, vmem, pl.BlockSpec(memory_space=pl.ANY)],
        out_specs=vmem,
        scratch_shapes=[
            pltpu.VMEM(listed.shape, jnp.int32),
            pltpu.SMEM(listed.shape, jnp.int32),
            held_cols,
            held_cols,
            pltpu.VMEM((4,) + group, jnp.float32),
            pltpu.VMEM((4,) + group, jnp.float32),
            pltpu.VMEM((2, 2) + group, jnp.float32),
            pltpu.VMEM((2,) + group, jnp.float32),
            pltpu.VMEM(group, jnp.float32),
            dma((n,)), dma((n,)), dma((n,)), dma((n,)),
            dma((2, 3)), dma((2, 3)), dma((2, 2)), dma((2, 2)), dma((2,)), dma((2,)), dma((2,)), dma,
        ],
        compiler_params=pltpu.CompilerParams(
            collective_id=0, has_side_effects=True, vmem_limit_bytes=56 << 20),
    )(listed, listed, sent)
    ids = lax.axis_index("tile") * quarter + jnp.arange(quarter, dtype=jnp.int32)
    return jnp.where((ids < tile_count)[:, None, None], held, 0.0)


def solution(mesh):
    owners, tile_size = mesh.devices.shape
    n = owners // PARTS
    assert n & (n - 1) == 0 and tile_size == 4
    split_mesh = Mesh(mesh.devices.reshape(PARTS, n, tile_size), ("part", "obs", "tile"))
    every = ("part", "obs", "tile")
    return jax.shard_map(
        functools.partial(body, n),
        mesh=split_mesh,
        in_specs=(P(every, None), P(every), P(), P(("part", "obs"), None, None), P(("part", "obs"))),
        out_specs=P(every, None, None),
        check_vma=False,
    )
```
